512 devices in a mesh: grid: 16 (over z, x_hi), recv: 32 (over x_lo, y, core).
Axes of the slice: x: 4 (x_hi: 2, x_lo: 2; x = x_hi * 2 + x_lo), y: 8, z: 8, core: 2. Of those that a mesh axis runs over, the one named last changes fastest.
Arguments:
- spectra: bfloat16 [2, 16, 20480], P(None, 'grid', 'recv'), may hold values from -6 to 6
- library: bfloat16 [16384, 2, 20480], P('grid', None, 'recv'), may hold values from -200 to 200, as said below
Outputs:
- power: float32 [16384], P(('grid', 'recv'))
The draws below stay inside these ranges and needn't reach their ends.
Inputs may be any that keep to these rules, and one draw needn't show every extreme that they name: `library`: finite values.
All inputs are finite; a program needn't handle non-finite values.
Results may differ from the reference program's by a relative error of at most 0.0003.
Values may be sent and summed in bfloat16 or wider, within the bound.
No kernel may reach another device: no remote copies, remote signals or barrier semaphores. Data moves between devices by JAX's collectives and lax.ppermute only.
A program may use at most 64 MiB of HBM per device.

```python
import math
import jax
import jax.numpy as jnp
from jax import lax

R = 20480
S = 16
GRID_DEV = 1024
P_SIZE = 16384


def draw_library(key, part):
    key = jax.random.fold_in(key, 1)
    k_col, k_row, k_elem = jax.random.split(key, 3)
    ramp = 1.0 + 2.0 * jnp.arange(R, dtype=jnp.float32) / (R - 1)
    column = jnp.exp(jax.random.uniform(k_col, (R,), jnp.float32, 0.0, math.log(10.0))) * ramp
    row = jnp.exp(jax.random.uniform(k_row, (P_SIZE,), jnp.float32, 0.0, math.log(10.0)))
    element = jnp.clip(jax.random.normal(k_elem, (P_SIZE, 2, R), jnp.float32), -4.0, 4.0)
    values = 0.1 * element * row[:, None, None] * column[None, None, :]
    return values.astype(jnp.bfloat16)


def block_scale(own_key, shape, shards, low, high):
    def one(position, parts):
        steps = jax.random.uniform(jax.random.fold_in(jax.random.fold_in(own_key, 6), position), (parts,), jnp.float32, low / len(shards), high / len(shards))
        return jnp.repeat(jnp.exp(steps), shape[position] // parts).reshape((-1,) + (1,) * (len(shape) - position - 1))

    factor_of = one(*shards[0])
    for cut in shards[1:]:
        factor_of = factor_of * one(*cut)
    return factor_of


def bell_draw(rng, dims, deviation, limit, pieces=(), kind=jnp.bfloat16):
    gain = block_scale(rng, dims, pieces, -0.22, 0.18) if pieces else 1.0
    drawn = jax.random.normal(rng, dims, jnp.float32) * deviation * gain
    return jnp.minimum(jnp.maximum(drawn, -limit), limit).astype(kind)


def setup_inputs(seed: int = 0) -> dict:
    seeds = jax.random.split(jax.random.key(seed), 3)
    spectra = bell_draw(seeds[0], (2, S, R), 1.0, 6.0, ((1, 16), (2, 32)))
    library = draw_library(jax.random.fold_in(seeds[2], 71), 0)
    return dict(spectra=spectra, library=library)


def stacked_spectra(spectra):
    real_part = spectra[0]
    imag_part = spectra[1]
    upper = jnp.concatenate([real_part, imag_part], axis=1)
    lower = jnp.concatenate([imag_part, -imag_part * 0 - real_part], axis=1)
    return jnp.concatenate([upper, lower], axis=0)


def reference(spectra, library):
    flat_lib = library.reshape(P_SIZE, 2 * R)
    stacked = stacked_spectra(spectra)
    beams = lax.dot_general(stacked, flat_lib, (((1,), (1,)), ((), ())), preferred_element_type=jnp.float32)
    blocks = library.reshape(P_SIZE // GRID_DEV, GRID_DEV, 2, R)

    def energy(block):
        wide = block.astype(jnp.float32)
        return jnp.sum(wide * wide, axis=(1, 2))

    weight = lax.map(energy, blocks).reshape(P_SIZE)
    total = jnp.sum(beams * beams, axis=0)
    return total / (S * (weight + 1e-6))
```

```python
import jax
import jax.numpy as jnp
from jax import lax
from jax.sharding import PartitionSpec as P


def shards(spectra, library):
    grid_size = lax.axis_size("grid")
    recv_size = lax.axis_size("recv")
    grid_rows = library.shape[0]
    recv_cols = library.shape[2]
    own_rows = grid_rows // recv_size
    snap_total = spectra.shape[1] * grid_size

    own = spectra.reshape(1, 2, recv_cols)
    piece = lax.all_to_all(
        jnp.broadcast_to(own, (grid_size, 2, recv_cols)), "grid", split_axis=0, concat_axis=0, tiled=True
    )
    real_part = piece[:, 0]
    imag_part = piece[:, 1]
    upper = jnp.concatenate([real_part, imag_part], axis=1)
    lower = jnp.concatenate([imag_part, -real_part], axis=1)
    stacked = jnp.concatenate([upper, lower], axis=0)
    flat_lib = library.reshape(grid_rows, 2 * recv_cols)
    product = lax.dot_general(
        stacked, flat_lib, (((1,), (1,)), ((), ())), preferred_element_type=jnp.float32
    )
    wide = library.astype(jnp.float32)
    energy = jnp.sum(wide * wide, axis=(1, 2))

    rows = jnp.concatenate([product, energy[None]], axis=0)
    blocks = rows.reshape(2 * snap_total + 1, recv_size, own_rows).transpose(1, 0, 2)
    blocks = blocks.reshape(recv_size, 1, (2 * snap_total + 1) * own_rows)
    arrived = lax.all_to_all(blocks, "recv", split_axis=0, concat_axis=0, tiled=True)
    summed = jnp.sum(arrived, axis=(0, 1)).reshape(2 * snap_total + 1, own_rows)
    beams = summed[: 2 * snap_total]
    total = jnp.sum(beams * beams, axis=0)
    weight = summed[2 * snap_total]
    return total / (snap_total * (weight + 1e-06))


def solution(mesh):
    placed = (P(None, "grid", "recv"), P("grid", None, "recv"))
    return jax.shard_map(
        shards, mesh=mesh, in_specs=placed, out_specs=P(("grid", "recv")), check_vma=False
    )
```

```python
import functools

import jax
import jax.numpy as jnp
from jax import lax
from jax.experimental import pallas as pl
from jax.experimental.pallas import tpu as pltpu
from jax.sharding import PartitionSpec as P

LANES = 128
SUB = 8
CHUNKS = 8
VMEM = pl.BlockSpec(memory_space=pltpu.VMEM)
PARAMS = pltpu.CompilerParams(vmem_limit_bytes=32 << 20)
NT = (((1,), (1,)), ((), ()))


def pieces(values):
    high = values.astype(jnp.bfloat16)
    rest = values - high.astype(jnp.float32)
    middle = rest.astype(jnp.bfloat16)
    low = (rest - middle.astype(jnp.float32)).astype(jnp.bfloat16)
    return high, middle, low


def split_kernel(lib_hbm, rows_ref, energy_ref, lib_ref, folded_ref, sems):
    owners, parts, sub, _, cols = lib_ref.shape
    tall = 2 * sub
    chunks = sems.shape[0]
    step = owners // chunks
    copies = [
        pltpu.make_async_copy(
            lib_hbm.at[pl.ds(chunk * step, step)], lib_ref.at[pl.ds(chunk * step, step)], sems.at[chunk]
        )
        for chunk in range(chunks)
    ]
    for copy in copies:
        copy.start()
    for chunk in range(chunks):
        copies[chunk].wait()
        for owner in range(chunk * step, (chunk + 1) * step):
            for part in range(parts):
                both = lib_ref[owner, part].reshape(tall, cols)
                rows_ref[part, owner * tall : (owner + 1) * tall, :] = both
                wide = both.astype(jnp.float32)
                square = wide * wide
                folded = square[:, :LANES]
                for start in range(LANES, cols, LANES):
                    folded = folded + square[:, start : start + LANES]
                folded_ref[part, owner * tall : (owner + 1) * tall, :] = folded
    target = lax.broadcasted_iota(jnp.int32, (LANES, LANES), 1)
    found = None
    for part in range(parts):
        ones = ((target >= part * sub) & (target < (part + 1) * sub)).astype(jnp.bfloat16)
        for piece in pieces(folded_ref[part]):
            term = jnp.dot(piece, ones, preferred_element_type=jnp.float32)
            found = term if found is None else found + term
    found = found.reshape(owners, tall, LANES)
    lane = lax.broadcasted_iota(jnp.int32, found.shape, 2)
    row = lax.broadcasted_iota(jnp.int32, found.shape, 1)
    energy_ref[...] = jnp.sum(jnp.where(lane % sub == row // 2, found, 0.0), axis=1)


def beam_kernel(spectra_ref, rows_ref, energy_ref, out_ref):
    parts, height, _ = rows_ref.shape
    tall = 2 * SUB
    owners = height // tall
    real = spectra_ref[:, 0, :]
    imag = spectra_ref[:, 1, :]
    with_real = jnp.concatenate([real, imag], axis=0)
    with_imag = jnp.concatenate([imag, -real], axis=0)
    zero = jnp.zeros_like(with_real)
    total = None
    for part in range(parts):
        placed = jnp.concatenate(
            [half if k == part else zero for half in (with_real, with_imag) for k in range(parts)], axis=0
        )
        term = lax.dot_general(rows_ref[part], placed, NT, preferred_element_type=jnp.float32)
        total = term if total is None else total + term
    even = lax.broadcasted_iota(jnp.int32, (SUB, LANES), 0) % 2 == 0
    for owner in range(owners):
        first = total[owner * tall : owner * tall + SUB]
        second = total[owner * tall + SUB : (owner + 1) * tall]
        of_real = jnp.where(even, first[:, :LANES], pltpu.roll(second[:, :LANES], 1, 0))
        of_imag = jnp.where(even, pltpu.roll(first[:, LANES:], SUB - 1, 0), second[:, LANES:])
        base = owner * (SUB + 1)
        out_ref[base : base + SUB, 0, :] = of_real + of_imag
        out_ref[base + SUB : base + SUB + 1, 0, :] = energy_ref[owner : owner + 1, :]


def power_kernel(snaps, arrived_ref, out_ref):
    height = SUB + 1
    senders = arrived_ref.shape[0] // height
    width = out_ref.shape[1] // SUB
    beams = arrived_ref[0:SUB, 0, :]
    weight = arrived_ref[SUB:height, 0, :]
    for sender in range(1, senders):
        base = sender * height
        beams = beams + arrived_ref[base : base + SUB, 0, :]
        weight = weight + arrived_ref[base + SUB : base + height, 0, :]
    source = lax.broadcasted_iota(jnp.int32, (LANES, LANES), 0)
    target = lax.broadcasted_iota(jnp.int32, (LANES, LANES), 1)
    same = (source // (LANES // width) == target // SUB).astype(jnp.bfloat16)
    stacked = jnp.concatenate(pieces(beams * beams), axis=0)
    found = jnp.dot(stacked, same, preferred_element_type=jnp.float32)
    found = found[:SUB] + found[SUB : 2 * SUB] + found[2 * SUB :]
    lane = lax.broadcasted_iota(jnp.int32, found.shape, 1)
    row = lax.broadcasted_iota(jnp.int32, found.shape, 0)
    point = (row // 2) + (row % 2) * (SUB // 2)
    total = jnp.sum(jnp.where(lane % SUB == point, found, 0.0), axis=0, keepdims=True)
    power = total / (snaps * (weight + 1e-06))
    out_ref[...] = power[:, : out_ref.shape[1]]


def shards(spectra, library):
    grid_size = lax.axis_size("grid")
    recv_size = lax.axis_size("recv")
    grid_rows = library.shape[0]
    recv_cols = library.shape[2]
    own_rows = grid_rows // recv_size
    snap_total = spectra.shape[1] * grid_size
    parts = own_rows // SUB
    height = SUB + 1

    own = spectra.reshape(1, 2, recv_cols)
    piece = lax.all_to_all(
        jnp.broadcast_to(own, (grid_size, 2, recv_cols)), "grid", split_axis=0, concat_axis=0, tiled=True
    )
    rows, energy = pl.pallas_call(
        split_kernel,
        out_shape=(
            jax.ShapeDtypeStruct((parts, recv_size * 2 * SUB, recv_cols), library.dtype),
            jax.ShapeDtypeStruct((recv_size, LANES), jnp.float32),
        ),
        in_specs=[pl.BlockSpec(memory_space=pltpu.HBM)],
        out_specs=(VMEM, VMEM),
        scratch_shapes=[
            pltpu.VMEM((recv_size, parts, SUB, 2, recv_cols), library.dtype),
            pltpu.VMEM((parts, recv_size * 2 * SUB, LANES), jnp.float32),
            pltpu.SemaphoreType.DMA((CHUNKS,)),
        ],
        compiler_params=PARAMS,
        cost_estimate=pl.CostEstimate(flops=4 * library.size, bytes_accessed=4 * library.size, transcendentals=0),
        name="split_rows",
    )(pltpu.with_memory_space_constraint(library.reshape(recv_size, parts, SUB, 2, recv_cols), pltpu.HBM))
    blocks = pl.pallas_call(
        beam_kernel,
        out_shape=jax.ShapeDtypeStruct((recv_size * height, 1, LANES), jnp.float32),
        in_specs=[VMEM, VMEM, VMEM],
        out_specs=VMEM,
        compiler_params=PARAMS,
        cost_estimate=pl.CostEstimate(
            flops=2 * library.size * 2 * snap_total, bytes_accessed=2 * library.size, transcendentals=0
        ),
        name="beams",
    )(piece, rows, energy)
    arrived = lax.all_to_all(blocks, "recv", split_axis=0, concat_axis=0, tiled=True)
    power = pl.pallas_call(
        functools.partial(power_kernel, snap_total),
        out_shape=jax.ShapeDtypeStruct((1, own_rows), jnp.float32),
        in_specs=[VMEM],
        out_specs=VMEM,
        compiler_params=PARAMS,
        name="power",
    )(arrived)
    return power.reshape(own_rows)


def solution(mesh):
    placed = (P(None, "grid", "recv"), P("grid", None, "recv"))
    return jax.shard_map(
        shards, mesh=mesh, in_specs=placed, out_specs=P(("grid", "recv")), check_vma=False
    )
```

```python
import functools

import jax
import jax.numpy as jnp
from jax import lax
from jax.experimental import pallas as pl
from jax.experimental.pallas import tpu as pltpu
from jax.sharding import PartitionSpec as P

LANES = 128
SUB = 8
CHUNKS = 8
EARLY = 6
VMEM = pl.BlockSpec(memory_space=pltpu.VMEM)
PARAMS = pltpu.CompilerParams(vmem_limit_bytes=32 << 20)
NT = (((1,), (1,)), ((), ()))


def pieces(values):
    high = values.astype(jnp.bfloat16)
    rest = values - high.astype(jnp.float32)
    middle = rest.astype(jnp.bfloat16)
    low = (rest - middle.astype(jnp.float32)).astype(jnp.bfloat16)
    return high, middle, low


def split_rows(slots, lib_hbm, rows_ref, energy_ref, lib_ref, folded_ref, sems):
    owners, parts, sub, _, cols = lib_ref.shape
    tall = 2 * sub
    chunks = sems.shape[0]
    step = owners // chunks
    copies = [
        pltpu.make_async_copy(
            lib_hbm.at[pl.ds(chunk * step, step)], lib_ref.at[pl.ds(chunk * step, step)], sems.at[chunk]
        )
        for chunk in range(chunks)
    ]
    for copy in copies:
        copy.start()
    for chunk in range(chunks):
        copies[chunk].wait()
        for owner in range(chunk * step, (chunk + 1) * step):
            base = slots[owner] * tall
            for part in range(parts):
                both = lib_ref[owner, part].reshape(tall, cols)
                rows_ref[part, base : base + tall, :] = both
                wide = both.astype(jnp.float32)
                square = wide * wide
                folded = square[:, :LANES]
                for start in range(LANES, cols, LANES):
                    folded = folded + square[:, start : start + LANES]
                folded_ref[part, base : base + tall, :] = folded
    target = lax.broadcasted_iota(jnp.int32, (LANES, LANES), 1)
    found = None
    for part in range(parts):
        ones = ((target >= part * sub) & (target < (part + 1) * sub)).astype(jnp.bfloat16)
        for piece in pieces(folded_ref[part]):
            term = jnp.dot(piece, ones, preferred_element_type=jnp.float32)
            found = term if found is None else found + term
    found = found.reshape(owners, tall, LANES)
    lane = lax.broadcasted_iota(jnp.int32, found.shape, 2)
    row = lax.broadcasted_iota(jnp.int32, found.shape, 1)
    energy_ref[...] = jnp.sum(jnp.where(lane % sub == row // 2, found, 0.0), axis=1)


def leaves_early():
    return lax.axis_index("grid") < EARLY


def prepare_kernel(slots, own_hbm, lib_hbm, out_ref, rows_ref, energy_ref, own_ref, lib_ref, folded_ref, sems, own_sem):
    copy = pltpu.make_async_copy(own_hbm, own_ref, own_sem)
    copy.start()
    copy.wait()
    own = own_ref[...]
    for target in range(out_ref.shape[0]):
        out_ref[target] = own

    @pl.when(leaves_early())
    def _():
        split_rows(slots, lib_hbm, rows_ref, energy_ref, lib_ref, folded_ref, sems)


def beams(spectra_ref, rows_ref, energy_ref, out_ref):
    parts, height, _ = rows_ref.shape
    tall = 2 * SUB
    owners = height // tall
    real = spectra_ref[:, 0, :]
    imag = spectra_ref[:, 1, :]
    with_real = jnp.concatenate([real, imag], axis=0)
    with_imag = jnp.concatenate([imag, -real], axis=0)
    zero = jnp.zeros_like(with_real)
    total = None
    for part in range(parts):
        placed = jnp.concatenate(
            [half if k == part else zero for half in (with_real, with_imag) for k in range(parts)], axis=0
        )
        term = lax.dot_general(rows_ref[part], placed, NT, preferred_element_type=jnp.float32)
        total = term if total is None else total + term
    even = lax.broadcasted_iota(jnp.int32, (SUB, LANES), 0) % 2 == 0
    for owner in range(owners):
        first = total[owner * tall : owner * tall + SUB]
        second = total[owner * tall + SUB : (owner + 1) * tall]
        of_real = jnp.where(even, first[:, :LANES], pltpu.roll(second[:, :LANES], 1, 0))
        of_imag = jnp.where(even, pltpu.roll(first[:, LANES:], SUB - 1, 0), second[:, LANES:])
        base = owner * (SUB + 1)
        out_ref[base : base + SUB, 0, :] = of_real + of_imag
        out_ref[base + SUB : base + SUB + 1, 0, :] = energy_ref[owner : owner + 1, :]


def beam_kernel(
    slots, spectra_ref, rows_ref, energy_ref, lib_hbm, out_ref, own_rows_ref, own_energy_ref, lib_ref, folded_ref, sems
):
    early = leaves_early()

    @pl.when(early)
    def _():
        beams(spectra_ref, rows_ref, energy_ref, out_ref)

    @pl.when(jnp.logical_not(early))
    def _():
        split_rows(slots, lib_hbm, own_rows_ref, own_energy_ref, lib_ref, folded_ref, sems)
        beams(spectra_ref, own_rows_ref, own_energy_ref, out_ref)


def power_kernel(snaps, arrived_ref, out_ref):
    height = SUB + 1
    senders = arrived_ref.shape[0] // height
    width = out_ref.shape[1] // SUB
    beams = arrived_ref[0:SUB, 0, :]
    weight = arrived_ref[SUB:height, 0, :]
    for sender in range(1, senders):
        base = sender * height
        beams = beams + arrived_ref[base : base + SUB, 0, :]
        weight = weight + arrived_ref[base + SUB : base + height, 0, :]
    source = lax.broadcasted_iota(jnp.int32, (LANES, LANES), 0)
    target = lax.broadcasted_iota(jnp.int32, (LANES, LANES), 1)
    same = (source // (LANES // width) == target // SUB).astype(jnp.bfloat16)
    stacked = jnp.concatenate(pieces(beams * beams), axis=0)
    found = jnp.dot(stacked, same, preferred_element_type=jnp.float32)
    found = found[:SUB] + found[SUB : 2 * SUB] + found[2 * SUB :]
    lane = lax.broadcasted_iota(jnp.int32, found.shape, 1)
    row = lax.broadcasted_iota(jnp.int32, found.shape, 0)
    point = (row // 2) + (row % 2) * (SUB // 2)
    total = jnp.sum(jnp.where(lane % SUB == point, found, 0.0), axis=0, keepdims=True)
    power = total / (snaps * (weight + 1e-06))
    out_ref[...] = power[:, : out_ref.shape[1]]


def exchange_orders(grid_size, recv_size):
    grid_order = list(range(grid_size))[::-1]
    line = recv_size // 2
    recv_order = [
        half + (pair + line // 2) % line + core
        for half in range(0, recv_size, line)
        for pair in range(0, line, 2)
        for core in (1, 0)
    ]
    return grid_order, recv_order


def shards(spectra, library):
    grid_size = lax.axis_size("grid")
    recv_size = lax.axis_size("recv")
    grid_rows = library.shape[0]
    recv_cols = library.shape[2]
    own_rows = grid_rows // recv_size
    snap_total = spectra.shape[1] * grid_size
    parts = own_rows // SUB
    height = SUB + 1
    grid_order, recv_order = exchange_orders(grid_size, recv_size)
    slots = [recv_order.index(owner) for owner in range(recv_size)]
    hbm = pl.BlockSpec(memory_space=pltpu.HBM)
    rows_shape = (parts, recv_size * 2 * SUB, recv_cols)
    energy_shape = (recv_size, LANES)
    scratch = [
        pltpu.VMEM((recv_size, parts, SUB, 2, recv_cols), library.dtype),
        pltpu.VMEM((parts, recv_size * 2 * SUB, LANES), jnp.float32),
        pltpu.SemaphoreType.DMA((CHUNKS,)),
    ]

    spectra = pltpu.with_memory_space_constraint(spectra.reshape(2, recv_cols), pltpu.HBM)
    library = pltpu.with_memory_space_constraint(
        library.reshape(recv_size, parts, SUB, 2, recv_cols), pltpu.HBM
    )
    own, rows, energy = pl.pallas_call(
        functools.partial(prepare_kernel, slots),
        out_shape=(
            jax.ShapeDtypeStruct((grid_size, 2, recv_cols), spectra.dtype),
            jax.ShapeDtypeStruct(rows_shape, library.dtype),
            jax.ShapeDtypeStruct(energy_shape, jnp.float32),
        ),
        in_specs=[hbm, hbm],
        out_specs=(VMEM, VMEM, VMEM),
        scratch_shapes=[pltpu.VMEM((2, recv_cols), spectra.dtype), *scratch, pltpu.SemaphoreType.DMA],
        compiler_params=PARAMS,
        name="prepare",
    )(spectra, library)
    piece = lax.all_to_all(
        own, "grid", split_axis=0, concat_axis=0, tiled=True, axis_index_groups=[grid_order]
    )
    blocks = pl.pallas_call(
        functools.partial(beam_kernel, slots),
        out_shape=jax.ShapeDtypeStruct((recv_size * height, 1, LANES), jnp.float32),
        in_specs=[VMEM, VMEM, VMEM, hbm],
        out_specs=VMEM,
        scratch_shapes=[pltpu.VMEM(rows_shape, library.dtype), pltpu.VMEM(energy_shape, jnp.float32), *scratch],
        compiler_params=PARAMS,
        name="beams",
    )(piece, rows, energy, library)
    arrived = lax.all_to_all(
        blocks, "recv", split_axis=0, concat_axis=0, tiled=True, axis_index_groups=[recv_order]
    )
    power = pl.pallas_call(
        functools.partial(power_kernel, snap_total),
        out_shape=jax.ShapeDtypeStruct((1, own_rows), jnp.float32),
        in_specs=[VMEM],
        out_specs=VMEM,
        compiler_params=PARAMS,
        name="power",
    )(arrived)
    return power.reshape(own_rows)


def solution(mesh):
    placed = (P(None, "grid", "recv"), P("grid", None, "recv"))
    return jax.shard_map(
        shards, mesh=mesh, in_specs=placed, out_specs=P(("grid", "recv")), check_vma=False
    )
```

```python
import functools

import jax
import jax.numpy as jnp
from jax import lax
from jax.experimental import pallas as pl
from jax.experimental.pallas import tpu as pltpu
from jax.sharding import PartitionSpec as P

LANES = 128
SUB = 8
CHUNKS = 8
EARLY = 6
VMEM = pl.BlockSpec(memory_space=pltpu.VMEM)
PARAMS = pltpu.CompilerParams(vmem_limit_bytes=32 << 20)
NT = (((1,), (1,)), ((), ()))


def pieces(values):
    high = values.astype(jnp.bfloat16)
    rest = values - high.astype(jnp.float32)
    middle = rest.astype(jnp.bfloat16)
    low = (rest - middle.astype(jnp.float32)).astype(jnp.bfloat16)
    return high, middle, low


def split_rows(slots, lib_hbm, rows_ref, energy_ref, lib_ref, folded_ref, sems):
    owners, parts, sub, _, cols = lib_ref.shape
    tall = 2 * sub
    chunks = sems.shape[0]
    step = owners // chunks
    copies = [
        pltpu.make_async_copy(
            lib_hbm.at[pl.ds(chunk * step, step)], lib_ref.at[pl.ds(chunk * step, step)], sems.at[chunk]
        )
        for chunk in range(chunks)
    ]
    for copy in copies:
        copy.start()
    for chunk in range(chunks):
        copies[chunk].wait()
        for owner in range(chunk * step, (chunk + 1) * step):
            base = slots[owner] * tall
            for part in range(parts):
                both = lib_ref[owner, part].reshape(tall, cols)
                side = part % 2 * cols
                rows_ref[part // 2, base : base + tall, side : side + cols] = both
                wide = both.astype(jnp.float32)
                square = wide * wide
                folded = square[:, :LANES]
                for start in range(LANES, cols, LANES):
                    folded = folded + square[:, start : start + LANES]
                folded_ref[part, base : base + tall, :] = folded
    target = lax.broadcasted_iota(jnp.int32, (LANES, LANES), 1)
    found = None
    for part in range(parts):
        ones = ((target >= part * sub) & (target < (part + 1) * sub)).astype(jnp.bfloat16)
        for piece in pieces(folded_ref[part]):
            term = jnp.dot(piece, ones, preferred_element_type=jnp.float32)
            found = term if found is None else found + term
    found = found.reshape(owners, tall, LANES)
    lane = lax.broadcasted_iota(jnp.int32, found.shape, 2)
    row = lax.broadcasted_iota(jnp.int32, found.shape, 1)
    energy_ref[...] = jnp.sum(jnp.where(lane % sub == row // 2, found, 0.0), axis=1)


def leaves_early():
    return lax.axis_index("grid") < EARLY


def prepare_kernel(slots, own_hbm, lib_hbm, out_ref, rows_ref, energy_ref, own_ref, lib_ref, folded_ref, sems, own_sem):
    copy = pltpu.make_async_copy(own_hbm, own_ref, own_sem)
    copy.start()
    copy.wait()
    own = own_ref[...]
    tiles = own.shape[1] // LANES
    for target in range(out_ref.shape[0] // tiles):
        for tile in range(tiles):
            out_ref[target * tiles + tile] = own[:, tile * LANES : (tile + 1) * LANES]

    @pl.when(leaves_early())
    def _():
        split_rows(slots, lib_hbm, rows_ref, energy_ref, lib_ref, folded_ref, sems)


def beams(spectra_ref, rows_ref, energy_ref, out_ref):
    pairs, height, _ = rows_ref.shape
    parts = 2 * pairs
    tall = 2 * SUB
    owners = height // tall
    tiles = rows_ref.shape[2] // (2 * LANES)
    snaps = spectra_ref.shape[0] // tiles
    by_tile = [spectra_ref[pl.ds(tile, snaps, stride=tiles)] for tile in range(tiles)]
    real = jnp.concatenate([block[:, 0, :] for block in by_tile], axis=1)
    imag = jnp.concatenate([block[:, 1, :] for block in by_tile], axis=1)
    with_real = jnp.concatenate([real, imag], axis=0)
    with_imag = jnp.concatenate([imag, -real], axis=0)
    zero = jnp.zeros_like(with_real)

    def placed(part):
        return jnp.concatenate(
            [half if k == part else zero for half in (with_real, with_imag) for k in range(parts)], axis=0
        )

    total = None
    for pair in range(pairs):
        weights = jnp.concatenate([placed(2 * pair), placed(2 * pair + 1)], axis=1)
        term = lax.dot_general(rows_ref[pair], weights, NT, preferred_element_type=jnp.float32)
        total = term if total is None else total + term
    even = lax.broadcasted_iota(jnp.int32, (SUB, LANES), 0) % 2 == 0
    for owner in range(owners):
        first = total[owner * tall : owner * tall + SUB]
        second = total[owner * tall + SUB : (owner + 1) * tall]
        of_real = jnp.where(even, first[:, :LANES], pltpu.roll(second[:, :LANES], 1, 0))
        of_imag = jnp.where(even, pltpu.roll(first[:, LANES:], SUB - 1, 0), second[:, LANES:])
        base = owner * (SUB + 1)
        out_ref[base : base + SUB, 0, :] = of_real + of_imag
        out_ref[base + SUB : base + SUB + 1, 0, :] = energy_ref[owner : owner + 1, :]


def beam_kernel(
    slots, spectra_ref, rows_ref, energy_ref, lib_hbm, out_ref, own_rows_ref, own_energy_ref, lib_ref, folded_ref, sems
):
    early = leaves_early()

    @pl.when(early)
    def _():
        beams(spectra_ref, rows_ref, energy_ref, out_ref)

    @pl.when(jnp.logical_not(early))
    def _():
        split_rows(slots, lib_hbm, own_rows_ref, own_energy_ref, lib_ref, folded_ref, sems)
        beams(spectra_ref, own_rows_ref, own_energy_ref, out_ref)


def power_kernel(snaps, arrived_ref, out_ref):
    height = SUB + 1
    senders = arrived_ref.shape[0] // height
    width = out_ref.shape[1] // SUB
    beams = arrived_ref[0:SUB, 0, :]
    weight = arrived_ref[SUB:height, 0, :]
    for sender in range(1, senders):
        base = sender * height
        beams = beams + arrived_ref[base : base + SUB, 0, :]
        weight = weight + arrived_ref[base + SUB : base + height, 0, :]
    source = lax.broadcasted_iota(jnp.int32, (LANES, LANES), 0)
    target = lax.broadcasted_iota(jnp.int32, (LANES, LANES), 1)
    same = (source // (LANES // width) == target // SUB).astype(jnp.bfloat16)
    stacked = jnp.concatenate(pieces(beams * beams), axis=0)
    found = jnp.dot(stacked, same, preferred_element_type=jnp.float32)
    found = found[:SUB] + found[SUB : 2 * SUB] + found[2 * SUB :]
    lane = lax.broadcasted_iota(jnp.int32, found.shape, 1)
    row = lax.broadcasted_iota(jnp.int32, found.shape, 0)
    point = (row // 2) + (row % 2) * (SUB // 2)
    total = jnp.sum(jnp.where(lane % SUB == point, found, 0.0), axis=0, keepdims=True)
    power = total / (snaps * (weight + 1e-06))
    out_ref[...] = power[:, : out_ref.shape[1]]


def exchange_orders(grid_size, recv_size):
    grid_order = list(range(grid_size))[::-1]
    line = recv_size // 2
    recv_order = [
        half + (pair + line // 2) % line + core
        for half in range(0, recv_size, line)
        for pair in range(0, line, 2)
        for core in (1, 0)
    ]
    return grid_order, recv_order


def shards(spectra, library):
    grid_size = lax.axis_size("grid")
    recv_size = lax.axis_size("recv")
    grid_rows = library.shape[0]
    recv_cols = library.shape[2]
    own_rows = grid_rows // recv_size
    snap_total = spectra.shape[1] * grid_size
    parts = own_rows // SUB
    height = SUB + 1
    grid_order, recv_order = exchange_orders(grid_size, recv_size)
    slots = [recv_order.index(owner) for owner in range(recv_size)]
    hbm = pl.BlockSpec(memory_space=pltpu.HBM)
    rows_shape = (parts // 2, recv_size * 2 * SUB, 2 * recv_cols)
    energy_shape = (recv_size, LANES)
    scratch = [
        pltpu.VMEM((recv_size, parts, SUB, 2, recv_cols), library.dtype),
        pltpu.VMEM((parts, recv_size * 2 * SUB, LANES), jnp.float32),
        pltpu.SemaphoreType.DMA((CHUNKS,)),
    ]

    spectra = pltpu.with_memory_space_constraint(spectra.reshape(2, recv_cols), pltpu.HBM)
    library = pltpu.with_memory_space_constraint(
        library.reshape(recv_size, parts, SUB, 2, recv_cols), pltpu.HBM
    )
    own, rows, energy = pl.pallas_call(
        functools.partial(prepare_kernel, slots),
        out_shape=(
            jax.ShapeDtypeStruct((grid_size * (recv_cols // LANES), 2, LANES), spectra.dtype),
            jax.ShapeDtypeStruct(rows_shape, library.dtype),
            jax.ShapeDtypeStruct(energy_shape, jnp.float32),
        ),
        in_specs=[hbm, hbm],
        out_specs=(VMEM, VMEM, VMEM),
        scratch_shapes=[pltpu.VMEM((2, recv_cols), spectra.dtype), *scratch, pltpu.SemaphoreType.DMA],
        compiler_params=PARAMS,
        name="prepare",
    )(spectra, library)
    piece = lax.all_to_all(
        own, "grid", split_axis=0, concat_axis=0, tiled=True, axis_index_groups=[grid_order]
    )
    blocks = pl.pallas_call(
        functools.partial(beam_kernel, slots),
        out_shape=jax.ShapeDtypeStruct((recv_size * height, 1, LANES), jnp.float32),
        in_specs=[VMEM, VMEM, VMEM, hbm],
        out_specs=VMEM,
        scratch_shapes=[pltpu.VMEM(rows_shape, library.dtype), pltpu.VMEM(energy_shape, jnp.float32), *scratch],
        compiler_params=PARAMS,
        name="beams",
    )(piece, rows, energy, library)
    arrived = lax.all_to_all(
        blocks, "recv", split_axis=0, concat_axis=0, tiled=True, axis_index_groups=[recv_order]
    )
    power = pl.pallas_call(
        functools.partial(power_kernel, snap_total),
        out_shape=jax.ShapeDtypeStruct((1, own_rows), jnp.float32),
        in_specs=[VMEM],
        out_specs=VMEM,
        compiler_params=PARAMS,
        name="power",
    )(arrived)
    return power.reshape(own_rows)


def solution(mesh):
    placed = (P(None, "grid", "recv"), P("grid", None, "recv"))
    return jax.shard_map(
        shards, mesh=mesh, in_specs=placed, out_specs=P(("grid", "recv")), check_vma=False
    )
```

```python
import functools

import jax
import jax.numpy as jnp
from jax import lax
from jax.experimental import pallas as pl
from jax.experimental.pallas import tpu as pltpu
from jax.sharding import PartitionSpec as P

LANES = 128
SUB = 8
CHUNKS = 8
EARLY = 6
WIDTH = 32
BLOCK = 5
TOP = 15
LOWEST = -14
VMEM = pl.BlockSpec(memory_space=pltpu.VMEM)
PARAMS = pltpu.CompilerParams(vmem_limit_bytes=32 << 20)
NT = (((1,), (1,)), ((), ()))


def pieces(values):
    high = values.astype(jnp.bfloat16)
    rest = values - high.astype(jnp.float32)
    middle = rest.astype(jnp.bfloat16)
    low = (rest - middle.astype(jnp.float32)).astype(jnp.bfloat16)
    return high, middle, low


def exponent(squares, highest):
    half = 0.5 * jnp.log2(jnp.maximum(squares, 1e-30)) + 0.01
    return jnp.clip(jnp.ceil(half), LOWEST, highest)


def point_of(row):
    return row // 2 + row % 2 * (SUB // 2)


def widen(points, first):
    owners = points.shape[0]
    shape = (owners, SUB, LANES)
    lane = lax.broadcasted_iota(jnp.int32, shape, 2)
    row = lax.broadcasted_iota(jnp.int32, shape, 1)
    own = (lane >= first) & (lane < first + WIDTH) & (lane % SUB == point_of(row))
    spread = jnp.where(own, jnp.broadcast_to(points[:, None, :], shape), 0.0)
    source = lax.broadcasted_iota(jnp.int32, (LANES, LANES), 0)
    target = lax.broadcasted_iota(jnp.int32, (LANES, LANES), 1)
    same = ((source - first) // SUB == target // WIDTH) & (source >= first)
    return jnp.dot(
        spread.reshape(owners * SUB, LANES).astype(jnp.bfloat16),
        same.astype(jnp.bfloat16),
        preferred_element_type=jnp.float32,
    )


def split_rows(slots, lib_hbm, rows_ref, tail_ref, lift_ref, lib_ref, folded_ref, sems):
    owners, parts, sub, _, cols = lib_ref.shape
    tall = 2 * sub
    chunks = sems.shape[0]
    step = owners // chunks
    copies = [
        pltpu.make_async_copy(
            lib_hbm.at[pl.ds(chunk * step, step)], lib_ref.at[pl.ds(chunk * step, step)], sems.at[chunk]
        )
        for chunk in range(chunks)
    ]
    for copy in copies:
        copy.start()
    for chunk in range(chunks):
        copies[chunk].wait()
        for owner in range(chunk * step, (chunk + 1) * step):
            base = slots[owner] * tall
            for part in range(parts):
                both = lib_ref[owner, part].reshape(tall, cols)
                side = part % 2 * cols
                rows_ref[part // 2, base : base + tall, side : side + cols] = both
                wide = both.astype(jnp.float32)
                square = wide * wide
                folded = square[:, :LANES]
                for start in range(LANES, cols, LANES):
                    folded = folded + square[:, start : start + LANES]
                folded_ref[part, base : base + tall, :] = folded
    target = lax.broadcasted_iota(jnp.int32, (LANES, LANES), 1)
    found = None
    for part in range(parts):
        ones = ((target >= part * sub) & (target < (part + 1) * sub)).astype(jnp.bfloat16)
        for piece in pieces(folded_ref[part]):
            term = jnp.dot(piece, ones, preferred_element_type=jnp.float32)
            found = term if found is None else found + term
    found = found.reshape(owners, tall, LANES)
    lane = lax.broadcasted_iota(jnp.int32, found.shape, 2)
    row = lax.broadcasted_iota(jnp.int32, found.shape, 1)
    energy = jnp.sum(jnp.where(lane % sub == row // 2, found, 0.0), axis=1)
    power = exponent(energy, 13)
    high, middle, low = pieces(jnp.sqrt(energy))
    lane = lax.broadcasted_iota(jnp.int32, energy.shape, 1)
    tail = jnp.where(lane < WIDTH, high.astype(jnp.float32), pltpu.roll(jnp.exp2(power), 3 * WIDTH, 1))
    tail = jnp.where(lane // WIDTH == 1, pltpu.roll(middle.astype(jnp.float32) * 2.0**8, WIDTH, 1), tail)
    tail = jnp.where(lane // WIDTH == 2, pltpu.roll(low.astype(jnp.float32) * 2.0**16, 2 * WIDTH, 1), tail)
    tail_ref[...] = tail
    lift_ref[...] = widen(jnp.exp2(TOP - power), 0)


def leaves_early():
    return lax.axis_index("grid") < EARLY


def prepare_kernel(slots, own_hbm, lib_hbm, out_ref, rows_ref, tail_ref, lift_ref, own_ref, lib_ref, folded_ref, sems, own_sem):
    copy = pltpu.make_async_copy(own_hbm, own_ref, own_sem)
    copy.start()
    copy.wait()
    own = own_ref[...]
    tiles = own.shape[1] // LANES
    for target in range(out_ref.shape[0] // tiles):
        for tile in range(tiles):
            out_ref[target * tiles + tile] = own[:, tile * LANES : (tile + 1) * LANES]

    @pl.when(leaves_early())
    def _():
        split_rows(slots, lib_hbm, rows_ref, tail_ref, lift_ref, lib_ref, folded_ref, sems)


def beams(spectra_ref, rows_ref, tail_ref, lift_ref, out_ref):
    pairs, height, _ = rows_ref.shape
    parts = 2 * pairs
    tall = 2 * SUB
    owners = height // tall
    tiles = rows_ref.shape[2] // (2 * LANES)
    snaps = spectra_ref.shape[0] // tiles
    by_tile = [spectra_ref[pl.ds(tile, snaps, stride=tiles)] for tile in range(tiles)]
    real = jnp.concatenate([block[:, 0, :] for block in by_tile], axis=1)
    imag = jnp.concatenate([block[:, 1, :] for block in by_tile], axis=1)
    with_real = jnp.concatenate([real, imag], axis=0)
    wide = with_real.astype(jnp.float32)
    squares = jnp.sum(jnp.sum(wide * wide, axis=0, keepdims=True), axis=1, keepdims=True)
    power = exponent(squares, 10)
    inverse = jnp.exp2(-power)
    scale = jnp.broadcast_to(jnp.exp2(power), (1, LANES))
    with_imag = jnp.concatenate([imag, -real], axis=0)
    zero = jnp.zeros_like(with_real)

    def placed(part):
        return jnp.concatenate(
            [half if k == part else zero for half in (with_real, with_imag) for k in range(parts)], axis=0
        )

    total = None
    for pair in range(pairs):
        weights = jnp.concatenate([placed(2 * pair), placed(2 * pair + 1)], axis=1)
        term = lax.dot_general(rows_ref[pair], weights, NT, preferred_element_type=jnp.float32)
        total = term if total is None else total + term
    even = lax.broadcasted_iota(jnp.int32, (SUB, LANES), 0) % 2 == 0
    for owner in range(owners):
        first = total[owner * tall : owner * tall + SUB]
        second = total[owner * tall + SUB : (owner + 1) * tall]
        of_real = jnp.where(even, first[:, :LANES], pltpu.roll(second[:, :LANES], 1, 0))
        of_imag = jnp.where(even, pltpu.roll(first[:, LANES:], SUB - 1, 0), second[:, LANES:])
        scaled = (of_real + of_imag) * (lift_ref[owner * SUB : (owner + 1) * SUB] * inverse)
        base = owner * BLOCK
        for pair in range(SUB // 2):
            out_ref[base + pair] = scaled[2 * pair : 2 * pair + 2]
        out_ref[base + SUB // 2, 0:1, :] = tail_ref[owner : owner + 1]
        out_ref[base + SUB // 2, 1:2, :] = scale


def beam_kernel(
    slots, spectra_ref, rows_ref, tail_ref, lift_ref, lib_hbm, out_ref, own_rows, own_tail, own_lift, lib_ref, folded_ref, sems
):
    early = leaves_early()

    @pl.when(early)
    def _():
        beams(spectra_ref, rows_ref, tail_ref, lift_ref, out_ref)

    @pl.when(jnp.logical_not(early))
    def _():
        split_rows(slots, lib_hbm, own_rows, own_tail, own_lift, lib_ref, folded_ref, sems)
        beams(spectra_ref, own_rows, own_tail, own_lift, out_ref)


def power_kernel(snaps, arrived_ref, out_ref):
    senders = arrived_ref.shape[0] // BLOCK
    width = out_ref.shape[1] // SUB
    tail = arrived_ref[pl.ds(SUB // 2, senders, stride=BLOCK), 0, :]
    scale = arrived_ref[pl.ds(SUB // 2, senders, stride=BLOCK), 1, :] * 2.0**-TOP
    root = tail + pltpu.roll(tail, 3 * WIDTH, 1) * 2.0**-8 + pltpu.roll(tail, 2 * WIDTH, 1) * 2.0**-16
    weight = jnp.sum(root * root, axis=0, keepdims=True)
    factor = widen(tail, 3 * WIDTH)
    beams = None
    for sender in range(senders):
        block = arrived_ref[sender * BLOCK : sender * BLOCK + SUB // 2].reshape(SUB, LANES)
        own = block * (factor[sender * SUB : (sender + 1) * SUB] * scale[sender : sender + 1])
        beams = own if beams is None else beams + own
    source = lax.broadcasted_iota(jnp.int32, (LANES, LANES), 0)
    target = lax.broadcasted_iota(jnp.int32, (LANES, LANES), 1)
    same = (source // (LANES // width) == target // SUB).astype(jnp.bfloat16)
    stacked = jnp.concatenate(pieces(beams * beams), axis=0)
    found = jnp.dot(stacked, same, preferred_element_type=jnp.float32)
    found = found[:SUB] + found[SUB : 2 * SUB] + found[2 * SUB :]
    lane = lax.broadcasted_iota(jnp.int32, found.shape, 1)
    row = lax.broadcasted_iota(jnp.int32, found.shape, 0)
    point = point_of(row)
    total = jnp.sum(jnp.where(lane % SUB == point, found, 0.0), axis=0, keepdims=True)
    power = total / (snaps * (weight + 1e-06))
    out_ref[...] = power[:, : out_ref.shape[1]]


def exchange_orders(grid_size, recv_size):
    grid_order = list(range(grid_size))[::-1]
    line = recv_size // 2
    recv_order = [
        half + (pair + line // 2) % line + core
        for half in range(0, recv_size, line)
        for pair in range(0, line, 2)
        for core in (1, 0)
    ]
    return grid_order, recv_order


def shards(spectra, library):
    grid_size = lax.axis_size("grid")
    recv_size = lax.axis_size("recv")
    grid_rows = library.shape[0]
    recv_cols = library.shape[2]
    own_rows = grid_rows // recv_size
    snap_total = spectra.shape[1] * grid_size
    parts = own_rows // SUB
    grid_order, recv_order = exchange_orders(grid_size, recv_size)
    slots = [recv_order.index(owner) for owner in range(recv_size)]
    hbm = pl.BlockSpec(memory_space=pltpu.HBM)
    rows_shape = (parts // 2, recv_size * 2 * SUB, 2 * recv_cols)
    tail_shape = (recv_size, LANES)
    lift_shape = (recv_size * SUB, LANES)
    scratch = [
        pltpu.VMEM((recv_size, parts, SUB, 2, recv_cols), library.dtype),
        pltpu.VMEM((parts, recv_size * 2 * SUB, LANES), jnp.float32),
        pltpu.SemaphoreType.DMA((CHUNKS,)),
    ]

    spectra = pltpu.with_memory_space_constraint(spectra.reshape(2, recv_cols), pltpu.HBM)
    library = pltpu.with_memory_space_constraint(
        library.reshape(recv_size, parts, SUB, 2, recv_cols), pltpu.HBM
    )
    own, rows, tail, lift = pl.pallas_call(
        functools.partial(prepare_kernel, slots),
        out_shape=(
            jax.ShapeDtypeStruct((grid_size * (recv_cols // LANES), 2, LANES), spectra.dtype),
            jax.ShapeDtypeStruct(rows_shape, library.dtype),
            jax.ShapeDtypeStruct(tail_shape, jnp.float32),
            jax.ShapeDtypeStruct(lift_shape, jnp.float32),
        ),
        in_specs=[hbm, hbm],
        out_specs=(VMEM, VMEM, VMEM, VMEM),
        scratch_shapes=[pltpu.VMEM((2, recv_cols), spectra.dtype), *scratch, pltpu.SemaphoreType.DMA],
        compiler_params=PARAMS,
        name="prepare",
    )(spectra, library)
    piece = lax.all_to_all(
        own, "grid", split_axis=0, concat_axis=0, tiled=True, axis_index_groups=[grid_order]
    )
    blocks = pl.pallas_call(
        functools.partial(beam_kernel, slots),
        out_shape=jax.ShapeDtypeStruct((recv_size * BLOCK, 2, LANES), jnp.float32),
        in_specs=[VMEM, VMEM, VMEM, VMEM, hbm],
        out_specs=VMEM,
        scratch_shapes=[pltpu.VMEM(rows_shape, library.dtype), pltpu.VMEM(tail_shape, jnp.float32), pltpu.VMEM(lift_shape, jnp.float32), *scratch],
        compiler_params=PARAMS,
        name="beams",
    )(piece, rows, tail, lift, library)
    arrived = lax.all_to_all(
        blocks.astype(jnp.float16), "recv", split_axis=0, concat_axis=0, tiled=True, axis_index_groups=[recv_order]
    )
    power = pl.pallas_call(
        functools.partial(power_kernel, snap_total),
        out_shape=jax.ShapeDtypeStruct((1, own_rows), jnp.float32),
        in_specs=[VMEM],
        out_specs=VMEM,
        compiler_params=PARAMS,
        name="power",
    )(arrived.astype(jnp.float32))
    return power.reshape(own_rows)


def solution(mesh):
    placed = (P(None, "grid", "recv"), P("grid", None, "recv"))
    return jax.shard_map(
        shards, mesh=mesh, in_specs=placed, out_specs=P(("grid", "recv")), check_vma=False
    )
```

```python
import functools

import jax
import jax.numpy as jnp
from jax import lax
from jax.experimental import pallas as pl
from jax.experimental.pallas import tpu as pltpu
from jax.sharding import PartitionSpec as P

LANES = 128
SUB = 8
CHUNKS = 8
EARLY = 6
WIDTH = 32
BLOCK = 5
TOP = 15
LOWEST = -14
VMEM = pl.BlockSpec(memory_space=pltpu.VMEM)
PARAMS = pltpu.CompilerParams(vmem_limit_bytes=32 << 20)
NT = (((1,), (1,)), ((), ()))


def pieces(values):
    high = values.astype(jnp.bfloat16)
    rest = values - high.astype(jnp.float32)
    middle = rest.astype(jnp.bfloat16)
    low = (rest - middle.astype(jnp.float32)).astype(jnp.bfloat16)
    return high, middle, low


def exponent(squares, highest):
    half = 0.5 * jnp.log2(jnp.maximum(squares, 1e-30)) + 0.01
    return jnp.clip(jnp.ceil(half), LOWEST, highest)


def point_of(row):
    return row // 2 + row % 2 * (SUB // 2)


def widen(points, first):
    owners = points.shape[0]
    shape = (owners, SUB, LANES)
    lane = lax.broadcasted_iota(jnp.int32, shape, 2)
    row = lax.broadcasted_iota(jnp.int32, shape, 1)
    own = (lane >= first) & (lane < first + WIDTH) & (lane % SUB == point_of(row))
    spread = jnp.where(own, jnp.broadcast_to(points[:, None, :], shape), 0.0)
    source = lax.broadcasted_iota(jnp.int32, (LANES, LANES), 0)
    target = lax.broadcasted_iota(jnp.int32, (LANES, LANES), 1)
    same = ((source - first) // SUB == target // WIDTH) & (source >= first)
    return jnp.dot(
        spread.reshape(owners * SUB, LANES).astype(jnp.bfloat16),
        same.astype(jnp.bfloat16),
        preferred_element_type=jnp.float32,
    )


def split_rows(slots, lib_hbm, rows_ref, tail_ref, lift_ref, lib_ref, folded_ref, sems):
    owners, parts, sub, _, cols = lib_ref.shape
    tall = 2 * sub
    chunks = sems.shape[0]
    step = owners // chunks
    copies = [
        pltpu.make_async_copy(
            lib_hbm.at[pl.ds(chunk * step, step)], lib_ref.at[pl.ds(chunk * step, step)], sems.at[chunk]
        )
        for chunk in range(chunks)
    ]
    for copy in copies:
        copy.start()
    for chunk in range(chunks):
        copies[chunk].wait()
        for owner in range(chunk * step, (chunk + 1) * step):
            base = slots[owner] * tall
            for part in range(parts):
                both = lib_ref[owner, part].reshape(tall, cols)
                side = part % 2 * cols
                rows_ref[part // 2, base : base + tall, side : side + cols] = both
                wide = both.astype(jnp.float32)
                square = wide * wide
                folded = square[:, :LANES]
                for start in range(LANES, cols, LANES):
                    folded = folded + square[:, start : start + LANES]
                folded_ref[part, base : base + tall, :] = folded
    target = lax.broadcasted_iota(jnp.int32, (LANES, LANES), 1)
    found = None
    for part in range(parts):
        ones = ((target >= part * sub) & (target < (part + 1) * sub)).astype(jnp.bfloat16)
        for piece in pieces(folded_ref[part]):
            term = jnp.dot(piece, ones, preferred_element_type=jnp.float32)
            found = term if found is None else found + term
    found = found.reshape(owners, tall, LANES)
    lane = lax.broadcasted_iota(jnp.int32, found.shape, 2)
    row = lax.broadcasted_iota(jnp.int32, found.shape, 1)
    energy = jnp.sum(jnp.where(lane % sub == row // 2, found, 0.0), axis=1)
    power = exponent(energy, 13)
    high, middle, low = pieces(jnp.sqrt(energy))
    lane = lax.broadcasted_iota(jnp.int32, energy.shape, 1)
    tail = jnp.where(lane < WIDTH, high.astype(jnp.float32), pltpu.roll(jnp.exp2(power), 3 * WIDTH, 1))
    tail = jnp.where(lane // WIDTH == 1, pltpu.roll(middle.astype(jnp.float32) * 2.0**8, WIDTH, 1), tail)
    tail = jnp.where(lane // WIDTH == 2, pltpu.roll(low.astype(jnp.float32) * 2.0**16, 2 * WIDTH, 1), tail)
    tail_ref[...] = tail
    lift_ref[...] = widen(jnp.exp2(TOP - power), 0)


def leaves_early():
    return lax.axis_index("grid") < EARLY


def prepare_kernel(slots, own_hbm, lib_hbm, out_ref, rows_ref, tail_ref, lift_ref, own_ref, lib_ref, folded_ref, sems, own_sem):
    copy = pltpu.make_async_copy(own_hbm, own_ref, own_sem)
    copy.start()
    copy.wait()
    own = own_ref[...]
    tiles = own.shape[1] // LANES
    for target in range(out_ref.shape[0] // tiles):
        for tile in range(tiles):
            out_ref[target * tiles + tile] = own[:, tile * LANES : (tile + 1) * LANES]

    @pl.when(leaves_early())
    def _():
        split_rows(slots, lib_hbm, rows_ref, tail_ref, lift_ref, lib_ref, folded_ref, sems)


def beams(spectra_ref, rows_ref, tail_ref, lift_ref, out_ref):
    pairs, height, _ = rows_ref.shape
    parts = 2 * pairs
    tall = 2 * SUB
    owners = height // tall
    tiles = rows_ref.shape[2] // (2 * LANES)
    snaps = spectra_ref.shape[0] // tiles
    by_tile = [spectra_ref[pl.ds(tile, snaps, stride=tiles)] for tile in range(tiles)]
    real = jnp.concatenate([block[:, 0, :] for block in by_tile], axis=1)
    imag = jnp.concatenate([block[:, 1, :] for block in by_tile], axis=1)
    with_real = jnp.concatenate([real, imag], axis=0)
    wide = with_real.astype(jnp.float32)
    squares = jnp.sum(jnp.sum(wide * wide, axis=0, keepdims=True), axis=1, keepdims=True)
    power = exponent(squares, 10)
    inverse = jnp.exp2(-power)
    scale = jnp.broadcast_to(jnp.exp2(power), (1, LANES))
    with_imag = jnp.concatenate([imag, -real], axis=0)
    zero = jnp.zeros_like(with_real)

    def placed(part):
        return jnp.concatenate(
            [half if k == part else zero for half in (with_real, with_imag) for k in range(parts)], axis=0
        )

    total = None
    for pair in range(pairs):
        weights = jnp.concatenate([placed(2 * pair), placed(2 * pair + 1)], axis=1)
        term = lax.dot_general(rows_ref[pair], weights, NT, preferred_element_type=jnp.float32)
        total = term if total is None else total + term
    even = lax.broadcasted_iota(jnp.int32, (SUB, LANES), 0) % 2 == 0
    for owner in range(owners):
        first = total[owner * tall : owner * tall + SUB]
        second = total[owner * tall + SUB : (owner + 1) * tall]
        of_real = jnp.where(even, first[:, :LANES], pltpu.roll(second[:, :LANES], 1, 0))
        of_imag = jnp.where(even, pltpu.roll(first[:, LANES:], SUB - 1, 0), second[:, LANES:])
        scaled = (of_real + of_imag) * (lift_ref[owner * SUB : (owner + 1) * SUB] * inverse)
        base = owner * BLOCK
        for pair in range(SUB // 2):
            out_ref[base + pair] = scaled[2 * pair : 2 * pair + 2]
        out_ref[base + SUB // 2, 0:1, :] = tail_ref[owner : owner + 1]
        out_ref[base + SUB // 2, 1:2, :] = scale


def beam_kernel(
    slots, spectra_ref, rows_ref, tail_ref, lift_ref, lib_hbm, out_ref, own_rows, own_tail, own_lift, lib_ref, folded_ref, sems
):
    early = leaves_early()

    @pl.when(early)
    def _():
        beams(spectra_ref, rows_ref, tail_ref, lift_ref, out_ref)

    @pl.when(jnp.logical_not(early))
    def _():
        split_rows(slots, lib_hbm, own_rows, own_tail, own_lift, lib_ref, folded_ref, sems)
        beams(spectra_ref, own_rows, own_tail, own_lift, out_ref)


def power_kernel(snaps, arrived_ref, out_ref):
    senders = arrived_ref.shape[0] // BLOCK
    width = out_ref.shape[1] // SUB
    tail = arrived_ref[pl.ds(SUB // 2, senders, stride=BLOCK), 0, :]
    scale = arrived_ref[pl.ds(SUB // 2, senders, stride=BLOCK), 1, :] * 2.0**-TOP
    root = tail + pltpu.roll(tail, 3 * WIDTH, 1) * 2.0**-8 + pltpu.roll(tail, 2 * WIDTH, 1) * 2.0**-16
    weight = jnp.sum(root * root, axis=0, keepdims=True)
    factor = widen(tail, 3 * WIDTH)
    beams = None
    for sender in range(senders):
        block = arrived_ref[sender * BLOCK : sender * BLOCK + SUB // 2].reshape(SUB, LANES)
        own = block * (factor[sender * SUB : (sender + 1) * SUB] * scale[sender : sender + 1])
        beams = own if beams is None else beams + own
    source = lax.broadcasted_iota(jnp.int32, (LANES, LANES), 0)
    target = lax.broadcasted_iota(jnp.int32, (LANES, LANES), 1)
    same = (source // (LANES // width) == target // SUB).astype(jnp.bfloat16)
    stacked = jnp.concatenate(pieces(beams * beams), axis=0)
    found = jnp.dot(stacked, same, preferred_element_type=jnp.float32)
    found = found[:SUB] + found[SUB : 2 * SUB] + found[2 * SUB :]
    lane = lax.broadcasted_iota(jnp.int32, found.shape, 1)
    row = lax.broadcasted_iota(jnp.int32, found.shape, 0)
    point = point_of(row)
    total = jnp.sum(jnp.where(lane % SUB == point, found, 0.0), axis=0, keepdims=True)
    power = total / (snaps * (weight + 1e-06))
    out_ref[...] = power[:, : out_ref.shape[1]]


def exchange_orders(grid_size, recv_size):
    grid_order = list(range(grid_size))[::-1]
    line = recv_size // 2
    ring = line // 2
    recv_order = [
        half + 2 * pair + core
        for pair in sorted(range(ring), key=lambda pair: min(pair, ring - pair))
        for half in (0, line)
        for core in (1, 0)
    ]
    last = line + 2 * (ring // 2) + 1
    recv_order.remove(last)
    recv_order.insert(0, last)
    return grid_order, recv_order


def shards(spectra, library):
    grid_size = lax.axis_size("grid")
    recv_size = lax.axis_size("recv")
    grid_rows = library.shape[0]
    recv_cols = library.shape[2]
    own_rows = grid_rows // recv_size
    snap_total = spectra.shape[1] * grid_size
    parts = own_rows // SUB
    grid_order, recv_order = exchange_orders(grid_size, recv_size)
    slots = [recv_order.index(owner) for owner in range(recv_size)]
    hbm = pl.BlockSpec(memory_space=pltpu.HBM)
    rows_shape = (parts // 2, recv_size * 2 * SUB, 2 * recv_cols)
    tail_shape = (recv_size, LANES)
    lift_shape = (recv_size * SUB, LANES)
    scratch = [
        pltpu.VMEM((recv_size, parts, SUB, 2, recv_cols), library.dtype),
        pltpu.VMEM((parts, recv_size * 2 * SUB, LANES), jnp.float32),
        pltpu.SemaphoreType.DMA((CHUNKS,)),
    ]

    spectra = pltpu.with_memory_space_constraint(spectra.reshape(2, recv_cols), pltpu.HBM)
    library = pltpu.with_memory_space_constraint(
        library.reshape(recv_size, parts, SUB, 2, recv_cols), pltpu.HBM
    )
    own, rows, tail, lift = pl.pallas_call(
        functools.partial(prepare_kernel, slots),
        out_shape=(
            jax.ShapeDtypeStruct((grid_size * (recv_cols // LANES), 2, LANES), spectra.dtype),
            jax.ShapeDtypeStruct(rows_shape, library.dtype),
            jax.ShapeDtypeStruct(tail_shape, jnp.float32),
            jax.ShapeDtypeStruct(lift_shape, jnp.float32),
        ),
        in_specs=[hbm, hbm],
        out_specs=(VMEM, VMEM, VMEM, VMEM),
        scratch_shapes=[pltpu.VMEM((2, recv_cols), spectra.dtype), *scratch, pltpu.SemaphoreType.DMA],
        compiler_params=PARAMS,
        name="prepare",
    )(spectra, library)
    piece = lax.all_to_all(
        own, "grid", split_axis=0, concat_axis=0, tiled=True, axis_index_groups=[grid_order]
    )
    blocks = pl.pallas_call(
        functools.partial(beam_kernel, slots),
        out_shape=jax.ShapeDtypeStruct((recv_size * BLOCK, 2, LANES), jnp.float32),
        in_specs=[VMEM, VMEM, VMEM, VMEM, hbm],
        out_specs=VMEM,
        scratch_shapes=[pltpu.VMEM(rows_shape, library.dtype), pltpu.VMEM(tail_shape, jnp.float32), pltpu.VMEM(lift_shape, jnp.float32), *scratch],
        compiler_params=PARAMS,
        name="beams",
    )(piece, rows, tail, lift, library)
    arrived = lax.all_to_all(
        blocks.astype(jnp.float16), "recv", split_axis=0, concat_axis=0, tiled=True, axis_index_groups=[recv_order]
    )
    power = pl.pallas_call(
        functools.partial(power_kernel, snap_total),
        out_shape=jax.ShapeDtypeStruct((1, own_rows), jnp.float32),
        in_specs=[VMEM],
        out_specs=VMEM,
        compiler_params=PARAMS,
        name="power",
    )(arrived.astype(jnp.float32))
    return power.reshape(own_rows)


def solution(mesh):
    placed = (P(None, "grid", "recv"), P("grid", None, "recv"))
    return jax.shard_map(
        shards, mesh=mesh, in_specs=placed, out_specs=P(("grid", "recv")), check_vma=False
    )
```

```python
import functools

import jax
import jax.numpy as jnp
from jax import lax
from jax.experimental import pallas as pl
from jax.experimental.pallas import tpu as pltpu
from jax.sharding import PartitionSpec as P

LANES = 128
SUB = 8
CHUNKS = 8
EARLY = 6
WIDTH = 32
BLOCK = 5
TOP = 15
LOWEST = -14
VMEM = pl.BlockSpec(memory_space=pltpu.VMEM)
PARAMS = pltpu.CompilerParams(vmem_limit_bytes=32 << 20)
NT = (((1,), (1,)), ((), ()))


def pieces(values):
    high = values.astype(jnp.bfloat16)
    rest = values - high.astype(jnp.float32)
    middle = rest.astype(jnp.bfloat16)
    low = (rest - middle.astype(jnp.float32)).astype(jnp.bfloat16)
    return high, middle, low


def exponent(squares, highest):
    half = 0.5 * jnp.log2(jnp.maximum(squares, 1e-30)) + 0.01
    return jnp.clip(jnp.ceil(half), LOWEST, highest)


def point_of(row):
    return row // 2 + row % 2 * (SUB // 2)


def widen(points, first):
    owners = points.shape[0]
    shape = (owners, SUB, LANES)
    lane = lax.broadcasted_iota(jnp.int32, shape, 2)
    row = lax.broadcasted_iota(jnp.int32, shape, 1)
    own = (lane >= first) & (lane < first + WIDTH) & (lane % SUB == point_of(row))
    spread = jnp.where(own, jnp.broadcast_to(points[:, None, :], shape), 0.0)
    source = lax.broadcasted_iota(jnp.int32, (LANES, LANES), 0)
    target = lax.broadcasted_iota(jnp.int32, (LANES, LANES), 1)
    same = ((source - first) // SUB == target // WIDTH) & (source >= first)
    return jnp.dot(
        spread.reshape(owners * SUB, LANES).astype(jnp.bfloat16),
        same.astype(jnp.bfloat16),
        preferred_element_type=jnp.float32,
    )


def split_rows(slots, lib_hbm, rows_ref, tail_ref, lift_ref, lib_ref, folded_ref, sems):
    owners, parts, sub, _, cols = lib_ref.shape
    tall = 2 * sub
    chunks = sems.shape[0]
    step = owners // chunks
    copies = [
        pltpu.make_async_copy(
            lib_hbm.at[pl.ds(chunk * step, step)], lib_ref.at[pl.ds(chunk * step, step)], sems.at[chunk]
        )
        for chunk in range(chunks)
    ]
    for copy in copies:
        copy.start()
    for chunk in range(chunks):
        copies[chunk].wait()
        for owner in range(chunk * step, (chunk + 1) * step):
            base = slots[owner] * tall
            for part in range(parts):
                both = lib_ref[owner, part].reshape(tall, cols)
                side = part % 2 * cols
                rows_ref[part // 2, base : base + tall, side : side + cols] = both
                wide = both.astype(jnp.float32)
                square = wide * wide
                folded = square[:, :LANES]
                for start in range(LANES, cols, LANES):
                    folded = folded + square[:, start : start + LANES]
                folded_ref[part, base : base + tall, :] = folded
    target = lax.broadcasted_iota(jnp.int32, (LANES, LANES), 1)
    found = None
    for part in range(parts):
        ones = ((target >= part * sub) & (target < (part + 1) * sub)).astype(jnp.bfloat16)
        for piece in pieces(folded_ref[part]):
            term = jnp.dot(piece, ones, preferred_element_type=jnp.float32)
            found = term if found is None else found + term
    found = found.reshape(owners, tall, LANES)
    lane = lax.broadcasted_iota(jnp.int32, found.shape, 2)
    row = lax.broadcasted_iota(jnp.int32, found.shape, 1)
    energy = jnp.sum(jnp.where(lane % sub == row // 2, found, 0.0), axis=1)
    power = exponent(energy, 13)
    high, middle, low = pieces(jnp.sqrt(energy))
    lane = lax.broadcasted_iota(jnp.int32, energy.shape, 1)
    tail = jnp.where(lane < WIDTH, high.astype(jnp.float32), pltpu.roll(jnp.exp2(power), 3 * WIDTH, 1))
    tail = jnp.where(lane // WIDTH == 1, pltpu.roll(middle.astype(jnp.float32) * 2.0**8, WIDTH, 1), tail)
    tail = jnp.where(lane // WIDTH == 2, pltpu.roll(low.astype(jnp.float32) * 2.0**16, 2 * WIDTH, 1), tail)
    tail_ref[...] = tail
    lift_ref[...] = widen(jnp.exp2(TOP - power), 0)


def leaves_early():
    return lax.axis_index("grid") < EARLY


def prepare_kernel(slots, own_hbm, lib_hbm, out_ref, rows_ref, tail_ref, lift_ref, own_ref, lib_ref, folded_ref, sems, own_sem):
    copy = pltpu.make_async_copy(own_hbm, own_ref, own_sem)
    copy.start()
    copy.wait()
    own = own_ref[...]
    tiles = own.shape[1] // LANES
    for target in range(out_ref.shape[0] // tiles):
        for tile in range(tiles):
            out_ref[target * tiles + tile] = own[:, tile * LANES : (tile + 1) * LANES]

    @pl.when(leaves_early())
    def _():
        split_rows(slots, lib_hbm, rows_ref, tail_ref, lift_ref, lib_ref, folded_ref, sems)


def beams(spectra_ref, rows_ref, tail_ref, lift_ref, out_ref):
    pairs, height, _ = rows_ref.shape
    parts = 2 * pairs
    tall = 2 * SUB
    owners = height // tall
    tiles = rows_ref.shape[2] // (2 * LANES)
    snaps = spectra_ref.shape[0] // tiles
    by_tile = [spectra_ref[pl.ds(tile, snaps, stride=tiles)] for tile in range(tiles)]
    real = jnp.concatenate([block[:, 0, :] for block in by_tile], axis=1)
    imag = jnp.concatenate([block[:, 1, :] for block in by_tile], axis=1)
    with_real = jnp.concatenate([real, imag], axis=0)
    wide = with_real.astype(jnp.float32)
    squares = jnp.sum(jnp.sum(wide * wide, axis=0, keepdims=True), axis=1, keepdims=True)
    power = exponent(squares, 10)
    inverse = jnp.exp2(-power)
    scale = jnp.broadcast_to(jnp.exp2(power), (1, LANES))
    with_imag = jnp.concatenate([imag, -real], axis=0)
    zero = jnp.zeros_like(with_real)

    def placed(part):
        return jnp.concatenate(
            [half if k == part else zero for half in (with_real, with_imag) for k in range(parts)], axis=0
        )

    total = None
    for pair in range(pairs):
        weights = jnp.concatenate([placed(2 * pair), placed(2 * pair + 1)], axis=1)
        term = lax.dot_general(rows_ref[pair], weights, NT, preferred_element_type=jnp.float32)
        total = term if total is None else total + term
    even = lax.broadcasted_iota(jnp.int32, (SUB, LANES), 0) % 2 == 0
    for owner in range(owners):
        first = total[owner * tall : owner * tall + SUB]
        second = total[owner * tall + SUB : (owner + 1) * tall]
        of_real = jnp.where(even, first[:, :LANES], pltpu.roll(second[:, :LANES], 1, 0))
        of_imag = jnp.where(even, pltpu.roll(first[:, LANES:], SUB - 1, 0), second[:, LANES:])
        scaled = (of_real + of_imag) * (lift_ref[owner * SUB : (owner + 1) * SUB] * inverse)
        base = owner * BLOCK
        for pair in range(SUB // 2):
            out_ref[base + pair] = scaled[2 * pair : 2 * pair + 2]
        out_ref[base + SUB // 2, 0:1, :] = tail_ref[owner : owner + 1]
        out_ref[base + SUB // 2, 1:2, :] = scale


def beam_kernel(
    slots, spectra_ref, rows_ref, tail_ref, lift_ref, lib_hbm, out_ref, own_rows, own_tail, own_lift, lib_ref, folded_ref, sems
):
    early = leaves_early()

    @pl.when(early)
    def _():
        beams(spectra_ref, rows_ref, tail_ref, lift_ref, out_ref)

    @pl.when(jnp.logical_not(early))
    def _():
        split_rows(slots, lib_hbm, own_rows, own_tail, own_lift, lib_ref, folded_ref, sems)
        beams(spectra_ref, own_rows, own_tail, own_lift, out_ref)


def power_kernel(snaps, arrived_ref, out_ref):
    senders = arrived_ref.shape[0] // BLOCK
    width = out_ref.shape[1] // SUB
    tail = arrived_ref[pl.ds(SUB // 2, senders, stride=BLOCK), 0, :]
    scale = arrived_ref[pl.ds(SUB // 2, senders, stride=BLOCK), 1, :] * 2.0**-TOP
    root = tail + pltpu.roll(tail, 3 * WIDTH, 1) * 2.0**-8 + pltpu.roll(tail, 2 * WIDTH, 1) * 2.0**-16
    weight = jnp.sum(root * root, axis=0, keepdims=True)
    factor = widen(tail * scale, 3 * WIDTH)
    beams = None
    for sender in range(senders):
        block = arrived_ref[sender * BLOCK : sender * BLOCK + SUB // 2].reshape(SUB, LANES)
        own = block * factor[sender * SUB : (sender + 1) * SUB]
        beams = own if beams is None else beams + own
    source = lax.broadcasted_iota(jnp.int32, (LANES, LANES), 0)
    target = lax.broadcasted_iota(jnp.int32, (LANES, LANES), 1)
    same = (source // (LANES // width) == target // SUB).astype(jnp.bfloat16)
    stacked = jnp.concatenate(pieces(beams * beams), axis=0)
    found = jnp.dot(stacked, same, preferred_element_type=jnp.float32)
    found = found[:SUB] + found[SUB : 2 * SUB] + found[2 * SUB :]
    lane = lax.broadcasted_iota(jnp.int32, found.shape, 1)
    row = lax.broadcasted_iota(jnp.int32, found.shape, 0)
    point = point_of(row)
    total = jnp.sum(jnp.where(lane % SUB == point, found, 0.0), axis=0, keepdims=True)
    power = total / (snaps * (weight + 1e-06))
    out_ref[...] = power[:, : out_ref.shape[1]]


def exchange_orders(grid_size, recv_size):
    grid_order = list(range(grid_size))[::-1]
    line = recv_size // 2
    ring = line // 2
    recv_order = [
        half + 2 * pair + core
        for pair in sorted(range(ring), key=lambda pair: min(pair, ring - pair))
        for half in (0, line)
        for core in (1, 0)
    ]
    last = line + 2 * (ring // 2) + 1
    recv_order.remove(last)
    recv_order.insert(0, last)
    return grid_order, recv_order


def shards(spectra, library):
    grid_size = lax.axis_size("grid")
    recv_size = lax.axis_size("recv")
    grid_rows = library.shape[0]
    recv_cols = library.shape[2]
    own_rows = grid_rows // recv_size
    snap_total = spectra.shape[1] * grid_size
    parts = own_rows // SUB
    grid_order, recv_order = exchange_orders(grid_size, recv_size)
    slots = [recv_order.index(owner) for owner in range(recv_size)]
    hbm = pl.BlockSpec(memory_space=pltpu.HBM)
    rows_shape = (parts // 2, recv_size * 2 * SUB, 2 * recv_cols)
    tail_shape = (recv_size, LANES)
    lift_shape = (recv_size * SUB, LANES)
    scratch = [
        pltpu.VMEM((recv_size, parts, SUB, 2, recv_cols), library.dtype),
        pltpu.VMEM((parts, recv_size * 2 * SUB, LANES), jnp.float32),
        pltpu.SemaphoreType.DMA((CHUNKS,)),
    ]

    spectra = pltpu.with_memory_space_constraint(spectra.reshape(2, recv_cols), pltpu.HBM)
    library = pltpu.with_memory_space_constraint(
        library.reshape(recv_size, parts, SUB, 2, recv_cols), pltpu.HBM
    )
    own, rows, tail, lift = pl.pallas_call(
        functools.partial(prepare_kernel, slots),
        out_shape=(
            jax.ShapeDtypeStruct((grid_size * (recv_cols // LANES), 2, LANES), spectra.dtype),
            jax.ShapeDtypeStruct(rows_shape, library.dtype),
            jax.ShapeDtypeStruct(tail_shape, jnp.float32),
            jax.ShapeDtypeStruct(lift_shape, jnp.float32),
        ),
        in_specs=[hbm, hbm],
        out_specs=(VMEM, VMEM, VMEM, VMEM),
        scratch_shapes=[pltpu.VMEM((2, recv_cols), spectra.dtype), *scratch, pltpu.SemaphoreType.DMA],
        compiler_params=PARAMS,
        name="prepare",
    )(spectra, library)
    piece = lax.all_to_all(
        own, "grid", split_axis=0, concat_axis=0, tiled=True, axis_index_groups=[grid_order]
    )
    blocks = pl.pallas_call(
        functools.partial(beam_kernel, slots),
        out_shape=jax.ShapeDtypeStruct((recv_size * BLOCK, 2, LANES), jnp.float32),
        in_specs=[VMEM, VMEM, VMEM, VMEM, hbm],
        out_specs=VMEM,
        scratch_shapes=[pltpu.VMEM(rows_shape, library.dtype), pltpu.VMEM(tail_shape, jnp.float32), pltpu.VMEM(lift_shape, jnp.float32), *scratch],
        compiler_params=PARAMS,
        name="beams",
    )(piece, rows, tail, lift, library)
    arrived = lax.all_to_all(
        blocks.astype(jnp.float16), "recv", split_axis=0, concat_axis=0, tiled=True, axis_index_groups=[recv_order]
    )
    power = pl.pallas_call(
        functools.partial(power_kernel, snap_total),
        out_shape=jax.ShapeDtypeStruct((1, own_rows), jnp.float32),
        in_specs=[VMEM],
        out_specs=VMEM,
        compiler_params=PARAMS,
        name="power",
    )(arrived.astype(jnp.float32))
    return power.reshape(own_rows)


def solution(mesh):
    placed = (P(None, "grid", "recv"), P("grid", None, "recv"))
    return jax.shard_map(
        shards, mesh=mesh, in_specs=placed, out_specs=P(("grid", "recv")), check_vma=False
    )
```

```python
import functools

import jax
import jax.numpy as jnp
from jax import lax
from jax.experimental import pallas as pl
from jax.experimental.pallas import tpu as pltpu
from jax.sharding import PartitionSpec as P

LANES = 128
SUB = 8
CHUNKS = 8
EARLY = 6
WIDTH = 32
BLOCK = 5
TOP = 15
LOWEST = -14
VMEM = pl.BlockSpec(memory_space=pltpu.VMEM)
PARAMS = pltpu.CompilerParams(vmem_limit_bytes=32 << 20)
NT = (((1,), (1,)), ((), ()))


def pieces(values):
    high = values.astype(jnp.bfloat16)
    rest = values - high.astype(jnp.float32)
    middle = rest.astype(jnp.bfloat16)
    low = (rest - middle.astype(jnp.float32)).astype(jnp.bfloat16)
    return high, middle, low


def exponent(squares, highest):
    half = 0.5 * jnp.log2(jnp.maximum(squares, 1e-30)) + 0.01
    return jnp.clip(jnp.ceil(half), LOWEST, highest)


def point_of(row):
    return row // 2 + row % 2 * (SUB // 2)


def widen(points, first):
    owners = points.shape[0]
    shape = (owners, SUB, LANES)
    lane = lax.broadcasted_iota(jnp.int32, shape, 2)
    row = lax.broadcasted_iota(jnp.int32, shape, 1)
    own = (lane >= first) & (lane < first + WIDTH) & (lane % SUB == point_of(row))
    spread = jnp.where(own, jnp.broadcast_to(points[:, None, :], shape), 0.0)
    source = lax.broadcasted_iota(jnp.int32, (LANES, LANES), 0)
    target = lax.broadcasted_iota(jnp.int32, (LANES, LANES), 1)
    same = ((source - first) // SUB == target // WIDTH) & (source >= first)
    return jnp.dot(
        spread.reshape(owners * SUB, LANES).astype(jnp.bfloat16),
        same.astype(jnp.bfloat16),
        preferred_element_type=jnp.float32,
    )


def split_rows(slots, lib_hbm, rows_ref, tail_ref, lift_ref, lib_ref, folded_ref, sems):
    owners, parts, sub, _, cols = lib_ref.shape
    tall = 2 * sub
    chunks = sems.shape[0]
    step = owners // chunks
    copies = [
        pltpu.make_async_copy(
            lib_hbm.at[pl.ds(chunk * step, step)], lib_ref.at[pl.ds(chunk * step, step)], sems.at[chunk]
        )
        for chunk in range(chunks)
    ]
    for copy in copies:
        copy.start()
    for chunk in range(chunks):
        copies[chunk].wait()
        for owner in range(chunk * step, (chunk + 1) * step):
            base = slots[owner] * tall
            for part in range(parts):
                both = lib_ref[owner, part].reshape(tall, cols)
                side = part % 2 * cols
                rows_ref[part // 2, base : base + tall, side : side + cols] = both
                wide = both.astype(jnp.float32)
                square = wide * wide
                folded = square[:, :LANES]
                for start in range(LANES, cols, LANES):
                    folded = folded + square[:, start : start + LANES]
                folded_ref[part, base : base + tall, :] = folded
    target = lax.broadcasted_iota(jnp.int32, (LANES, LANES), 1)
    found = None
    for part in range(parts):
        ones = ((target >= part * sub) & (target < (part + 1) * sub)).astype(jnp.bfloat16)
        for piece in pieces(folded_ref[part]):
            term = jnp.dot(piece, ones, preferred_element_type=jnp.float32)
            found = term if found is None else found + term
    found = found.reshape(owners, tall, LANES)
    lane = lax.broadcasted_iota(jnp.int32, found.shape, 2)
    row = lax.broadcasted_iota(jnp.int32, found.shape, 1)
    energy = jnp.sum(jnp.where(lane % sub == row // 2, found, 0.0), axis=1)
    power = exponent(energy, 13)
    high, middle, low = pieces(jnp.sqrt(energy))
    lane = lax.broadcasted_iota(jnp.int32, energy.shape, 1)
    tail = jnp.where(lane < WIDTH, high.astype(jnp.float32), pltpu.roll(jnp.exp2(power), 3 * WIDTH, 1))
    tail = jnp.where(lane // WIDTH == 1, pltpu.roll(middle.astype(jnp.float32) * 2.0**8, WIDTH, 1), tail)
    tail = jnp.where(lane // WIDTH == 2, pltpu.roll(low.astype(jnp.float32) * 2.0**16, 2 * WIDTH, 1), tail)
    tail_ref[...] = tail
    lift_ref[...] = widen(jnp.exp2(TOP - power), 0)


def leaves_early():
    return lax.axis_index("grid") < EARLY


def prepare_kernel(slots, own_hbm, lib_hbm, out_ref, rows_ref, tail_ref, lift_ref, own_ref, lib_ref, folded_ref, sems, own_sem):
    copy = pltpu.make_async_copy(own_hbm, own_ref, own_sem)
    copy.start()
    copy.wait()
    own = own_ref[...]
    tiles = own.shape[1] // LANES
    for target in range(out_ref.shape[0] // tiles):
        for tile in range(tiles):
            out_ref[target * tiles + tile] = own[:, tile * LANES : (tile + 1) * LANES]

    @pl.when(leaves_early())
    def _():
        split_rows(slots, lib_hbm, rows_ref, tail_ref, lift_ref, lib_ref, folded_ref, sems)


def beams(spectra_ref, rows_ref, tail_ref, lift_ref, out_ref):
    pairs, height, _ = rows_ref.shape
    parts = 2 * pairs
    tall = 2 * SUB
    owners = height // tall
    tiles = rows_ref.shape[2] // (2 * LANES)
    snaps = spectra_ref.shape[0] // tiles
    by_tile = [spectra_ref[pl.ds(tile, snaps, stride=tiles)] for tile in range(tiles)]
    real = jnp.concatenate([block[:, 0, :] for block in by_tile], axis=1)
    imag = jnp.concatenate([block[:, 1, :] for block in by_tile], axis=1)
    with_real = jnp.concatenate([real, imag], axis=0)
    wide = with_real.astype(jnp.float32)
    squares = jnp.sum(jnp.sum(wide * wide, axis=0, keepdims=True), axis=1, keepdims=True)
    power = exponent(squares, 10)
    inverse = jnp.exp2(-power)
    scale = jnp.broadcast_to(jnp.exp2(power), (1, LANES))
    with_imag = jnp.concatenate([imag, -real], axis=0)
    zero = jnp.zeros_like(with_real)

    def placed(part):
        return jnp.concatenate(
            [half if k == part else zero for half in (with_real, with_imag) for k in range(parts)], axis=0
        )

    total = None
    for pair in range(pairs):
        weights = jnp.concatenate([placed(2 * pair), placed(2 * pair + 1)], axis=1)
        term = lax.dot_general(rows_ref[pair], weights, NT, preferred_element_type=jnp.float32)
        total = term if total is None else total + term
    even = lax.broadcasted_iota(jnp.int32, (SUB, LANES), 0) % 2 == 0
    for owner in range(owners):
        first = total[owner * tall : owner * tall + SUB]
        second = total[owner * tall + SUB : (owner + 1) * tall]
        of_real = jnp.where(even, first[:, :LANES], pltpu.roll(second[:, :LANES], 1, 0))
        of_imag = jnp.where(even, pltpu.roll(first[:, LANES:], SUB - 1, 0), second[:, LANES:])
        scaled = (of_real + of_imag) * (lift_ref[owner * SUB : (owner + 1) * SUB] * inverse)
        base = owner * BLOCK
        for pair in range(SUB // 2):
            out_ref[base + pair] = scaled[2 * pair : 2 * pair + 2]
        out_ref[base + SUB // 2, 0:1, :] = tail_ref[owner : owner + 1]
        out_ref[base + SUB // 2, 1:2, :] = scale


def beam_kernel(
    slots, spectra_ref, rows_ref, tail_ref, lift_ref, lib_hbm, out_ref, own_rows, own_tail, own_lift, lib_ref, folded_ref, sems
):
    early = leaves_early()

    @pl.when(early)
    def _():
        beams(spectra_ref, rows_ref, tail_ref, lift_ref, out_ref)

    @pl.when(jnp.logical_not(early))
    def _():
        split_rows(slots, lib_hbm, own_rows, own_tail, own_lift, lib_ref, folded_ref, sems)
        beams(spectra_ref, own_rows, own_tail, own_lift, out_ref)


def power_kernel(snaps, arrived_ref, out_ref):
    senders = arrived_ref.shape[0] // BLOCK
    width = out_ref.shape[1] // SUB
    tail = arrived_ref[pl.ds(SUB // 2, senders, stride=BLOCK), 0, :]
    scale = arrived_ref[pl.ds(SUB // 2, senders, stride=BLOCK), 1, :] * 2.0**-TOP
    root = tail + pltpu.roll(tail, 3 * WIDTH, 1) * 2.0**-8 + pltpu.roll(tail, 2 * WIDTH, 1) * 2.0**-16
    weight = jnp.sum(root * root, axis=0, keepdims=True)
    factor = widen(tail, 3 * WIDTH)
    beams = None
    for sender in range(senders):
        block = arrived_ref[sender * BLOCK : sender * BLOCK + SUB // 2].reshape(SUB, LANES)
        own = block * (factor[sender * SUB : (sender + 1) * SUB] * scale[sender : sender + 1])
        beams = own if beams is None else beams + own
    source = lax.broadcasted_iota(jnp.int32, (LANES, LANES), 0)
    target = lax.broadcasted_iota(jnp.int32, (LANES, LANES), 1)
    same = (source // (LANES // width) == target // SUB).astype(jnp.bfloat16)
    stacked = jnp.concatenate(pieces(beams * beams), axis=0)
    found = jnp.dot(stacked, same, preferred_element_type=jnp.float32)
    found = found[:SUB] + found[SUB : 2 * SUB] + found[2 * SUB :]
    lane = lax.broadcasted_iota(jnp.int32, found.shape, 1)
    row = lax.broadcasted_iota(jnp.int32, found.shape, 0)
    point = point_of(row)
    total = jnp.sum(jnp.where(lane % SUB == point, found, 0.0), axis=0, keepdims=True)
    power = total / (snaps * (weight + 1e-06))
    out_ref[...] = power[:, : out_ref.shape[1]]


def exchange_orders(grid_size, recv_size):
    grid_order = [grid_size - 3, *(place for place in range(grid_size)[::-1] if place != grid_size - 3)]
    line = recv_size // 2
    ring = line // 2
    recv_order = [
        half + 2 * pair + core
        for pair in sorted(range(ring), key=lambda pair: min(pair, ring - pair))
        for half in (0, line)
        for core in (1, 0)
    ]
    last = line + 2 * (ring // 2) + 1
    recv_order.remove(last)
    recv_order.insert(0, last)
    return grid_order, recv_order


def shards(spectra, library):
    grid_size = lax.axis_size("grid")
    recv_size = lax.axis_size("recv")
    grid_rows = library.shape[0]
    recv_cols = library.shape[2]
    own_rows = grid_rows // recv_size
    snap_total = spectra.shape[1] * grid_size
    parts = own_rows // SUB
    grid_order, recv_order = exchange_orders(grid_size, recv_size)
    slots = [recv_order.index(owner) for owner in range(recv_size)]
    hbm = pl.BlockSpec(memory_space=pltpu.HBM)
    rows_shape = (parts // 2, recv_size * 2 * SUB, 2 * recv_cols)
    tail_shape = (recv_size, LANES)
    lift_shape = (recv_size * SUB, LANES)
    scratch = [
        pltpu.VMEM((recv_size, parts, SUB, 2, recv_cols), library.dtype),
        pltpu.VMEM((parts, recv_size * 2 * SUB, LANES), jnp.float32),
        pltpu.SemaphoreType.DMA((CHUNKS,)),
    ]

    spectra = pltpu.with_memory_space_constraint(spectra.reshape(2, recv_cols), pltpu.HBM)
    library = pltpu.with_memory_space_constraint(
        library.reshape(recv_size, parts, SUB, 2, recv_cols), pltpu.HBM
    )
    own, rows, tail, lift = pl.pallas_call(
        functools.partial(prepare_kernel, slots),
        out_shape=(
            jax.ShapeDtypeStruct((grid_size * (recv_cols // LANES), 2, LANES), spectra.dtype),
            jax.ShapeDtypeStruct(rows_shape, library.dtype),
            jax.ShapeDtypeStruct(tail_shape, jnp.float32),
            jax.ShapeDtypeStruct(lift_shape, jnp.float32),
        ),
        in_specs=[hbm, hbm],
        out_specs=(VMEM, VMEM, VMEM, VMEM),
        scratch_shapes=[pltpu.VMEM((2, recv_cols), spectra.dtype), *scratch, pltpu.SemaphoreType.DMA],
        compiler_params=PARAMS,
        name="prepare",
    )(spectra, library)
    piece = lax.all_to_all(
        own, "grid", split_axis=0, concat_axis=0, tiled=True, axis_index_groups=[grid_order]
    )
    blocks = pl.pallas_call(
        functools.partial(beam_kernel, slots),
        out_shape=jax.ShapeDtypeStruct((recv_size * BLOCK, 2, LANES), jnp.float32),
        in_specs=[VMEM, VMEM, VMEM, VMEM, hbm],
        out_specs=VMEM,
        scratch_shapes=[pltpu.VMEM(rows_shape, library.dtype), pltpu.VMEM(tail_shape, jnp.float32), pltpu.VMEM(lift_shape, jnp.float32), *scratch],
        compiler_params=PARAMS,
        name="beams",
    )(piece, rows, tail, lift, library)
    arrived = lax.all_to_all(
        blocks.astype(jnp.float16), "recv", split_axis=0, concat_axis=0, tiled=True, axis_index_groups=[recv_order]
    )
    power = pl.pallas_call(
        functools.partial(power_kernel, snap_total),
        out_shape=jax.ShapeDtypeStruct((1, own_rows), jnp.float32),
        in_specs=[VMEM],
        out_specs=VMEM,
        compiler_params=PARAMS,
        name="power",
    )(arrived.astype(jnp.float32))
    return power.reshape(own_rows)


def solution(mesh):
    placed = (P(None, "grid", "recv"), P("grid", None, "recv"))
    return jax.shard_map(
        shards, mesh=mesh, in_specs=placed, out_specs=P(("grid", "recv")), check_vma=False
    )
```
